32 devices in a mesh: groups: 2 (over y), az: 4 (over z), rad: 2 (over x), vert: 2 (over core).
Axes of the slice: x: 2, y: 2, z: 4, core: 2. Of those that a mesh axis runs over, the one named last changes fastest.
Arguments:
- state: float32 [16, 8, 64, 512], P('groups', 'vert', 'rad', 'az'), parts along dimension 0, as said below
- orbit_shift: int32 [128], P(('groups', 'rad')), parts along dimension 0, may hold values from 0 to 511
- remap_shift: int32 [2], P('groups'), parts along dimension 0, may hold values from 0 to 511
Outputs:
- state_new: float32 [16, 8, 64, 512], P('groups', 'vert', 'rad', 'az'), parts along dimension 0
The draws below stay inside these ranges and needn't reach their ends.
There are 2 independent parts, one for each index of `groups`. The reference program is written for one: setup_inputs(seed, part) draws one part's arguments, and reference() takes and returns one part's arrays. A program takes and returns all parts, laid end to end along the dimension named above; each array names one. Nothing has to cross between parts.
Inputs may be any that keep to these rules, and one draw needn't show every extreme that they name: Every cell of state has positive density and positive gas pressure.
All inputs are finite; a program needn't handle non-finite values.
Results may differ from the reference program's by a relative error of at most 0.00002.
Values sent between devices are 32-bit elements; how exact they have to be, the bound alone decides.
A program may use at most 128 MiB of HBM per device.

```python
import jax
import jax.numpy as jnp
from jax import lax

NR = 64
NA = 512
NV = 8


def draw_state(key, part):
    key = jax.random.fold_in(key, 11)
    subkeys = jax.random.split(key, 4)
    grid_shape = (NV, NR, NA)
    density = jnp.exp(jax.random.uniform(subkeys[0], grid_shape, jnp.float32, -0.693, 0.693))
    velocity = 0.5 * jax.random.truncated_normal(subkeys[1], -3.0, 3.0, (3,) + grid_shape, jnp.float32)
    magnet = 0.5 * jax.random.truncated_normal(subkeys[2], -3.0, 3.0, (3,) + grid_shape, jnp.float32)
    pressure = jnp.exp(jax.random.uniform(subkeys[3], grid_shape, jnp.float32, -0.693, 0.693))
    momentum = density[None] * velocity
    energy = 1.5 * pressure + 0.5 * jnp.sum(momentum * velocity, axis=0) + 0.5 * jnp.sum(magnet * magnet, axis=0)
    return jnp.concatenate([density[None], momentum, energy[None], magnet], axis=0).astype(jnp.float32)


def place_ends(values, key, least, top_value):
    index_at = [jax.random.randint(jax.random.fold_in(key, axis), (), 0, length) for axis, length in enumerate(values.shape)]
    main_axis = values.shape.index(max(values.shape))
    neighbour = index_at[:main_axis] + [(index_at[main_axis] + 1) % values.shape[main_axis]] + index_at[main_axis + 1:]
    return values.at[tuple(index_at)].set(least).at[tuple(neighbour)].set(top_value)


def setup_inputs(seed: int = 0, part: int = 0) -> dict:
    key_list = jax.random.split(jax.random.key(seed), 4)
    part_keys = jax.random.split(jax.random.fold_in(key_list[3], part), 4)
    return {
        "state": draw_state(jax.random.fold_in(jax.random.fold_in(key_list[3], part), 71), part),
        "orbit_shift": place_ends(jax.random.randint(part_keys[1], (NR,), 0, NA), jax.random.fold_in(part_keys[1], 1), 0, NA - 1).astype(jnp.int32),
        "remap_shift": jax.random.randint(part_keys[2], (1,), 0, NA).astype(jnp.int32),
    }


ADIABATIC = 5.0 / 3.0
TIME_STEP = 0.125
ROTATION = 1.0
SHEAR_RATE = 1.5

def normal_flux(cells, normal):
    density = cells[0]
    momentum = cells[1:4]
    energy = cells[4]
    magnet = cells[5:8]
    velocity = momentum / density
    magnet_sq = lax.optimization_barrier(jnp.sum(magnet * magnet, axis=0))
    kinetic = 0.5 * lax.optimization_barrier(jnp.sum(momentum * velocity, axis=0))
    pressure = (ADIABATIC - 1.0) * (energy - kinetic - 0.5 * magnet_sq)
    total_pressure = pressure + 0.5 * magnet_sq
    normal_speed = velocity[normal]
    normal_field = magnet[normal]
    projection = lax.optimization_barrier(jnp.sum(velocity * magnet, axis=0))
    pieces = [density * normal_speed]
    for component in range(3):
        term = momentum[component] * normal_speed - magnet[component] * normal_field
        if component == normal:
            term = term + total_pressure
        pieces.append(term)
    pieces.append((energy + total_pressure) * normal_speed - normal_field * projection)
    for component in range(3):
        pieces.append(magnet[component] * normal_speed - velocity[component] * normal_field)
    fast_speed = jnp.sqrt((ADIABATIC * pressure + magnet_sq) / density)
    return (jnp.stack(pieces), normal_speed, fast_speed)

def riemann_flux(left_cells, right_cells, normal):
    left_flux, left_speed, left_fast = normal_flux(left_cells, normal)
    right_flux, right_speed, right_fast = normal_flux(right_cells, normal)
    slow_bound = jnp.minimum(jnp.minimum(left_speed - left_fast, right_speed - right_fast), 0.0)
    fast_bound = jnp.maximum(jnp.maximum(left_speed + left_fast, right_speed + right_fast), 0.0)
    return (fast_bound * left_flux - slow_bound * right_flux + slow_bound * fast_bound * (right_cells - left_cells)) / (fast_bound - slow_bound)

def advance(padded):
    flux_x = riemann_flux(padded[:, :, :-1, :], padded[:, :, 1:, :], 0)
    flux_y = riemann_flux(padded[:, :, :, :-1], padded[:, :, :, 1:], 1)
    flux_z = riemann_flux(padded[:, :-1], padded[:, 1:], 2)
    interior = padded[:, 1:-1, 1:-1, 1:-1]
    change = flux_x[:, 1:-1, 1:, 1:-1] - flux_x[:, 1:-1, :-1, 1:-1] + (flux_y[:, 1:-1, 1:-1, 1:] - flux_y[:, 1:-1, 1:-1, :-1]) + (flux_z[:, 1:, 1:-1, 1:-1] - flux_z[:, :-1, 1:-1, 1:-1])
    hydro_new = interior[:5] - TIME_STEP * change[:5]
    xflux_by = flux_x[6, 1:-1]
    yflux_bx = flux_y[5, 1:-1]
    emf_z = 0.25 * (yflux_bx[:, 1:, :] + yflux_bx[:, :-1, :] - (xflux_by[:, :, 1:] + xflux_by[:, :, :-1]))
    xflux_bz = flux_x[7, :, :, 1:-1]
    zflux_bx = flux_z[5, :, :, 1:-1]
    emf_y = 0.25 * (xflux_bz[1:] + xflux_bz[:-1] - (zflux_bx[:, 1:] + zflux_bx[:, :-1]))
    yflux_bz = flux_y[7, :, 1:-1, :]
    zflux_by = flux_z[6, :, 1:-1, :]
    emf_x = 0.25 * (zflux_by[:, :, 1:] + zflux_by[:, :, :-1] - (yflux_bz[1:] + yflux_bz[:-1]))
    ez_mid_x = 0.5 * (emf_z[:, 1:] + emf_z[:, :-1])
    ez_mid_y = 0.5 * (emf_z[:, :, 1:] + emf_z[:, :, :-1])
    ey_mid_x = 0.5 * (emf_y[:, 1:] + emf_y[:, :-1])
    ey_mid_z = 0.5 * (emf_y[1:] + emf_y[:-1])
    ex_mid_y = 0.5 * (emf_x[:, :, 1:] + emf_x[:, :, :-1])
    ex_mid_z = 0.5 * (emf_x[1:] + emf_x[:-1])
    field_x = interior[5] - TIME_STEP * (ez_mid_x[:, :, 1:] - ez_mid_x[:, :, :-1] - (ey_mid_x[1:] - ey_mid_x[:-1]))
    field_y = interior[6] - TIME_STEP * (ex_mid_y[1:] - ex_mid_y[:-1] - (ez_mid_y[:, 1:] - ez_mid_y[:, :-1]))
    field_z = interior[7] - TIME_STEP * (ey_mid_z[:, 1:] - ey_mid_z[:, :-1] - (ex_mid_z[:, :, 1:] - ex_mid_z[:, :, :-1]))
    momentum_x = hydro_new[1] + TIME_STEP * 2.0 * ROTATION * interior[2]
    momentum_y = hydro_new[2] + TIME_STEP * (SHEAR_RATE - 2.0) * ROTATION * interior[1]
    return jnp.stack([hydro_new[0], momentum_x, momentum_y, hydro_new[3], hydro_new[4], field_x, field_y, field_z])

def reference(state, orbit_shift, remap_shift):
    cycle_cells = state.shape[3]
    columns = jnp.arange(cycle_cells, dtype=jnp.int32)
    positions = jnp.mod(columns[None, :] - orbit_shift[:, None].astype(jnp.int32), cycle_cells).astype(jnp.int32)
    moved = jnp.take_along_axis(state, jnp.broadcast_to(positions[None, None], state.shape), axis=3)
    shear_offset = remap_shift[0]
    inner_ghost = jnp.roll(moved[:, :, -1:, :], shear_offset, axis=3)
    outer_ghost = jnp.roll(moved[:, :, :1, :], -shear_offset, axis=3)
    extended = jnp.concatenate([inner_ghost, moved, outer_ghost], axis=2)
    extended = jnp.concatenate([extended[..., -1:], extended, extended[..., :1]], axis=3)
    extended = jnp.concatenate([extended[:, -1:], extended, extended[:, :1]], axis=1)
    return advance(extended)
```

```python
import functools

import jax
import jax.numpy as jnp
from jax import lax
from jax.experimental import pallas as pl
from jax.experimental.pallas import tpu as pltpu
from jax.sharding import PartitionSpec as P

ADIABATIC = 5.0 / 3.0
TIME_STEP = 0.125
ROTATION = 1.0
SHEAR_RATE = 1.5
MESH = pl.DeviceIdType.MESH
LANES = 128


def lane_index(shape):
    return lax.broadcasted_iota(jnp.int32, shape, len(shape) - 1)


def pair_of_step(step, per, planes):
    if per % planes == 0 and planes == 4:
        fields = per // planes
        return (step % fields) * planes + (3 * (step // fields)) % planes
    return step


def move_kernel(
    count,
    rads,
    state,
    shift,
    main,
    ghost_cols,
    ghost_rows,
    side_cols,
    z_main,
    z_cols,
    z_rows,
    z_side,
    rows,
    turned,
    out_cols,
    out_rows,
    send1,
    recv1,
    send2,
    recv2,
    send3,
    recv3,
    send4,
    recv4,
    own_sem,
):
    fields, planes, height, _ = main.shape
    per = fields * planes // count
    group = lax.axis_index("groups")
    me = lax.axis_index("az")
    rad = lax.axis_index("rad")
    core = lax.axis_index("vert")
    up = (rad + 1) % rads
    down = (rad + rads - 1) % rads

    def device(az, r, v):
        return (group, az, r, v)

    barrier = pltpu.get_barrier_semaphore()
    targets = [device((me + d) % count, rad, core) for d in range(1, count)]
    for d in range(count):
        targets.append(device((me + d) % count, up, core))
        if rads > 2:
            targets.append(device((me + d) % count, down, core))
    targets.append(device(me, rad, 1 - core))
    for target in targets:
        pl.semaphore_signal(barrier, inc=1, device_id=target, device_id_type=MESH)
    pl.semaphore_wait(barrier, len(targets))

    def first(step, d):
        pair = pair_of_step(step, per, planes)
        peer = (me + d) % count
        return pltpu.make_async_remote_copy(
            src_ref=state.at[peer * per + pair],
            dst_ref=rows.at[me, pair],
            send_sem=send1.at[step, d],
            recv_sem=recv1.at[step, d],
            device_id=device(peer, rad, core),
            device_id_type=MESH,
        )

    def second(step, d):
        pair = pair_of_step(step, per, planes)
        peer = (me + d) % count
        whole = me * per + pair
        return pltpu.make_async_remote_copy(
            src_ref=turned.at[peer, pair],
            dst_ref=main.at[whole // planes, whole % planes],
            send_sem=send2.at[step, d],
            recv_sem=recv2.at[step, d],
            device_id=device(peer, rad, core),
            device_id_type=MESH,
        )

    own = pltpu.make_async_copy(state.at[pl.ds(me * per, per)], rows.at[me], own_sem.at[0])
    own.start()

    def start_first(step, carry):
        for d in range(1, count):
            first(step, d).start()
        return carry

    lax.fori_loop(0, per, start_first, 0)
    out_cols[...] = jnp.zeros_like(out_cols)
    own.wait()

    tiles = height // 8
    bits = []
    total = count * LANES
    bit = 0
    while (1 << bit) < total:
        bits.append(bit)
        bit += 1

    def turn(step, carry):
        pair = pair_of_step(step, per, planes)
        for d in range(1, count):
            first(step, d).wait_recv()
        lane8 = lane_index((8, LANES))
        sub8 = lax.broadcasted_iota(jnp.int32, (8, LANES), 0)
        for t in range(tiles + 1):
            amount = shift[pl.ds(8 * t, 8), :]
            if t < tiles:
                blocks = [rows[b, pair, pl.ds(8 * t, 8), :] for b in range(count)]
            else:
                blocks = [
                    jnp.where(
                        sub8 == 7,
                        rows[b, pair, pl.ds(height - 1, 1), :],
                        rows[b, pair, pl.ds(0, 1), :],
                    )
                    for b in range(count)
                ]
            for bit in bits:
                if (1 << bit) < LANES:
                    continue
                q = (1 << bit) // LANES
                flag = ((amount >> bit) & 1) == 1
                blocks = [
                    jnp.where(flag, blocks[(b - q) % count], blocks[b]) for b in range(count)
                ]
            for bit in bits:
                if (1 << bit) >= LANES:
                    continue
                flag = ((amount >> bit) & 1) == 1
                blocks = [
                    jnp.where(flag, pltpu.roll(block, 1 << bit, 1), block) for block in blocks
                ]
            inside = lane8 >= (amount & (LANES - 1))
            out = [
                jnp.where(inside, blocks[b], blocks[(b - 1) % count]) for b in range(count)
            ]
            place = 2 * per * t + 2 * pair
            for b in range(count):
                low = jnp.broadcast_to(out[(b - 1) % count][:, LANES - 1 :], (8, LANES))
                high = jnp.broadcast_to(out[(b + 1) % count][:, :1], (8, LANES))
                out_cols[b] = jnp.where(
                    lane8 == place, low, jnp.where(lane8 == place + 1, high, out_cols[b])
                )
                if t < tiles:
                    turned[b, pair, pl.ds(8 * t, 8), :] = out[b]
                else:
                    out_rows[b, 0, pl.ds(pair, 1), :] = out[b][0:1]
                    out_rows[b, 1, pl.ds(pair, 1), :] = out[b][7:8]
        for d in range(1, count):
            second(step, d).start()
        whole = me * per + pair
        main[whole // planes, whole % planes] = turned[me, pair]
        return carry

    lax.fori_loop(0, per, turn, 0)

    late = []
    for d in range(count):
        peer = (me + d) % count
        if d > 0:
            late.append(
                pltpu.make_async_remote_copy(
                    src_ref=out_cols.at[peer],
                    dst_ref=ghost_cols.at[me],
                    send_sem=send3.at[d],
                    recv_sem=recv3.at[d],
                    device_id=device(peer, rad, core),
                    device_id_type=MESH,
                )
            )
        for side, r in ((0, down), (1, up)):
            slot = count + d * 4 + side * 2
            late.append(
                pltpu.make_async_remote_copy(
                    src_ref=out_rows.at[peer, side],
                    dst_ref=ghost_rows.at[side, me],
                    send_sem=send3.at[slot],
                    recv_sem=recv3.at[slot],
                    device_id=device(peer, r, core),
                    device_id_type=MESH,
                )
            )
            late.append(
                pltpu.make_async_remote_copy(
                    src_ref=out_cols.at[peer],
                    dst_ref=side_cols.at[side, me],
                    send_sem=send3.at[slot + 1],
                    recv_sem=recv3.at[slot + 1],
                    device_id=device(peer, r, core),
                    device_id_type=MESH,
                )
            )
    for copy in late:
        copy.start()
    ghost_cols[me] = out_cols[me]

    def wait_second(step, carry):
        for d in range(1, count):
            second(step, d).wait_recv()
        return carry

    def across(index, source, target):
        return pltpu.make_async_remote_copy(
            src_ref=source,
            dst_ref=target,
            send_sem=send4.at[index],
            recv_sem=recv4.at[index],
            device_id=device(me, rad, 1 - core),
            device_id_type=MESH,
        )

    early = per // 2 if per % planes == 0 and planes == 4 else per
    lax.fori_loop(0, early, wait_second, 0)
    last = [
        across(0, main.at[:, planes - 1], z_main.at[0]),
        across(1, main.at[:, 0], z_main.at[1]),
    ]
    for copy in last:
        copy.start()
    for copy in late:
        copy.wait_recv()
    more = [
        across(2, ghost_cols, z_cols),
        across(3, ghost_rows, z_rows),
        across(4, side_cols, z_side),
    ]
    for copy in more:
        copy.start()
    if early < per:
        lax.fori_loop(early, per, wait_second, 0)
    for copy in last + more:
        copy.wait()

    def finish(step, carry):
        for d in range(1, count):
            first(step, d).wait_send()
            second(step, d).wait_send()
        return carry

    lax.fori_loop(0, per, finish, 0)
    for copy in late:
        copy.wait_send()


def primitives(cells):
    density, mx, my, mz, energy, bx, by, bz = cells
    inverse = 1.0 / density
    velocity = (mx * inverse, my * inverse, mz * inverse)
    magnet_sq = bx * bx + by * by + bz * bz
    kinetic = 0.5 * (mx * velocity[0] + my * velocity[1] + mz * velocity[2])
    pressure = (ADIABATIC - 1.0) * (energy - kinetic - 0.5 * magnet_sq)
    total_pressure = pressure + 0.5 * magnet_sq
    projection = velocity[0] * bx + velocity[1] * by + velocity[2] * bz
    fast_speed = jnp.sqrt((ADIABATIC * pressure + magnet_sq) * inverse)
    return velocity, total_pressure, projection, fast_speed


def one_flux(cells, prims, normal, piece):
    velocity, total_pressure, projection, _ = prims
    speed = velocity[normal]
    field = cells[5 + normal]
    if piece == 0:
        return cells[1 + normal]
    if piece < 4:
        value = cells[piece] * speed - cells[piece + 4] * field
        return value + total_pressure if piece == normal + 1 else value
    if piece == 4:
        return (cells[4] + total_pressure) * speed - field * projection
    return cells[piece] * speed - velocity[piece - 5] * field


def face_flux(left, left_prims, right, right_prims, normal, pieces):
    ls, lc = left_prims[0][normal], left_prims[3]
    rs, rc = right_prims[0][normal], right_prims[3]
    low = jnp.minimum(jnp.minimum(ls - lc, rs - rc), 0.0)
    high = jnp.maximum(jnp.maximum(ls + lc, rs + rc), 0.0)
    inverse = 1.0 / (high - low)
    wl = high * inverse
    wr = low * inverse
    wd = low * wl
    out = []
    for piece in pieces:
        if piece == 5 + normal:
            out.append(wd * (right[piece] - left[piece]))
            continue
        out.append(
            wl * one_flux(left, left_prims, normal, piece)
            - wr * one_flux(right, right_prims, normal, piece)
            + wd * (right[piece] - left[piece])
        )
    return out


def step_kernel(
    count,
    main,
    ghost_cols,
    ghost_rows,
    side_cols,
    z_main,
    z_cols,
    z_rows,
    z_side,
    new,
    pad,
    cols,
    edge,
    fx7,
    fy7,
    fyr7,
    change,
    curl,
    zface,
    gy,
    gx6,
    gz6,
):
    fields, planes, height, _ = main.shape
    per = fields * planes // count
    tiles = height // 8
    tall = height + 8
    lane8 = lane_index((8, LANES))
    sub8 = lax.broadcasted_iota(jnp.int32, (8, LANES), 0)
    lane = lane_index((tall, LANES))
    padded = planes + 2

    for f in range(fields):
        for p in range(padded):
            k = (p - 1) % planes
            owner, slot = divmod(f * planes + k, per)
            if 1 <= p <= planes:
                pad[p, f, pl.ds(0, height)] = main[f, k]
                edge_rows = ghost_rows
            else:
                pad[p, f, pl.ds(0, height)] = z_main[0 if p == 0 else 1, f]
                edge_rows = z_rows
            pad[p, f, pl.ds(height, 8)] = jnp.where(
                sub8 == 7,
                edge_rows[1, owner, pl.ds(slot, 1), :],
                edge_rows[0, owner, pl.ds(slot, 1), :],
            )
        for t in range(tiles + 1):
            tile = jnp.ones((8, LANES), jnp.float32)
            for p in range(padded):
                k = (p - 1) % planes
                owner, slot = divmod(f * planes + k, per)
                inner = 1 <= p <= planes
                if t < tiles:
                    source = (ghost_cols if inner else z_cols)[owner]
                else:
                    both = side_cols if inner else z_side
                    source = jnp.where(sub8 == 7, both[1, owner], both[0, owner])
                moved = pltpu.roll(source, (2 * p - 2 * per * t - 2 * slot) % LANES, 1)
                tile = jnp.where(lane8 // 2 == p, moved, tile)
            cols[f, pl.ds(8 * t, 8)] = tile
        tile = jnp.ones((tall, LANES), jnp.float32)
        for p in range(padded):
            tile = jnp.where(lane // 2 == p, pltpu.roll(pad[p, f], 2 * p + 2, 1), tile)
        edge[f] = tile

    def below(x):
        return pltpu.roll(x, 1, 0)

    def above(x):
        return pltpu.roll(x, tall - 1, 0)

    ghost = [cols[f] for f in range(fields)]
    ghost_prims = primitives(ghost)
    last = [edge[f] for f in range(fields)]
    for piece, value in enumerate(
        face_flux(last, primitives(last), ghost, ghost_prims, 1, range(8))
    ):
        gy[piece] = value
    lower = [below(x) for x in ghost]
    gx6[...] = face_flux(lower, primitives(lower), ghost, ghost_prims, 0, (6,))[0]
    higher = [pltpu.roll(x, LANES - 2, 1) for x in ghost]
    gz6[...] = face_flux(ghost, ghost_prims, higher, primitives(higher), 2, (6,))[0]

    def left_of(x, ghosts, p):
        return jnp.where(lane == 0, pltpu.roll(ghosts, LANES - 2 * p, 1), pltpu.roll(x, 1, 1))

    def right_of(x, ghosts, p):
        return jnp.where(
            lane == LANES - 1,
            pltpu.roll(ghosts, LANES - 2 - 2 * p, 1),
            pltpu.roll(x, LANES - 1, 1),
        )

    def in_plane(p, carry):
        cells = [pad[p, f] for f in range(fields)]
        prims = primitives(cells)
        lower = [below(x) for x in cells]
        flux = face_flux(lower, primitives(lower), cells, prims, 0, range(8))
        fx7[p] = flux[7]
        for f in range(5):
            change[p, f] = (above(flux[f]) - flux[f])[:height]
        x6 = flux[6]
        side = [left_of(cells[f], cols[f], p) for f in range(fields)]
        flux = face_flux(side, primitives(side), cells, prims, 1, range(8))
        fy7[p] = flux[7]
        fyr7[p] = right_of(flux[7], gy[7], p)
        for f in range(5):
            change[p, f] += (right_of(flux[f], gy[f], p) - flux[f])[:height]
        y5 = flux[5]
        y5r = right_of(y5, gy[5], p)
        x6l = left_of(x6, gx6[...], p)
        x6r = right_of(x6, gx6[...], p)
        ez = 0.25 * (y5 + below(y5) - (x6 + x6l))
        ezr = 0.25 * (y5r + below(y5r) - (x6r + x6))
        ez_up = above(ez)
        ezr_up = above(ezr)
        curl[p, 0] = (0.5 * ((ezr_up + ezr) - (ez_up + ez)))[:height]
        curl[p, 1] = (0.5 * ((ezr_up + ez_up) - (ezr + ez)))[:height]
        return carry

    lax.fori_loop(0, padded, in_plane, 0)

    def between(q, carry):
        low = [pad[q, f] for f in range(fields)]
        high = [pad[q + 1, f] for f in range(fields)]
        flux = face_flux(low, primitives(low), high, primitives(high), 2, range(8))
        for f in range(5):
            zface[q, f] = flux[f][:height]
        z5, z6 = flux[5], flux[6]
        ey = 0.25 * (fx7[q + 1] + fx7[q] - (z5 + below(z5)))
        ex = 0.25 * (z6 + left_of(z6, gz6[...], q) - (fy7[q + 1] + fy7[q]))
        exr = 0.25 * (right_of(z6, gz6[...], q) + z6 - (fyr7[q + 1] + fyr7[q]))
        ey_up = above(ey)
        zface[q, 5] = (0.5 * (ey_up + ey))[:height]
        zface[q, 6] = (0.5 * (exr + ex))[:height]
        zface[q, 7] = (0.5 * ((ey_up - ey) - (exr - ex)))[:height]
        return carry

    lax.fori_loop(0, planes + 1, between, 0)

    def combine(k, carry):
        p = k + 1
        old = [pad[p, f, pl.ds(0, height)] for f in range(fields)]
        hydro = [
            old[f] - TIME_STEP * (change[p, f] + (zface[p, f] - zface[k, f])) for f in range(5)
        ]
        new[0, k] = hydro[0]
        new[1, k] = hydro[1] + TIME_STEP * 2.0 * ROTATION * old[2]
        new[2, k] = hydro[2] + TIME_STEP * (SHEAR_RATE - 2.0) * ROTATION * old[1]
        new[3, k] = hydro[3]
        new[4, k] = hydro[4]
        new[5, k] = old[5] - TIME_STEP * (curl[p, 0] - (zface[p, 5] - zface[k, 5]))
        new[6, k] = old[6] - TIME_STEP * ((zface[p, 6] - zface[k, 6]) - curl[p, 1])
        new[7, k] = old[7] - TIME_STEP * (zface[p, 7] + zface[k, 7])
        return carry

    lax.fori_loop(0, planes, combine, 0)


def per_device(state, orbit_shift, remap_shift):
    count = lax.axis_size("az")
    rads = lax.axis_size("rad")
    fields, planes, height, width = state.shape
    total = count * width
    per = fields * planes // count
    rad = lax.axis_index("rad")
    offset = remap_shift[0]
    top = jnp.where(rad == rads - 1, offset, 0)
    bottom = jnp.where(rad == 0, total - offset, 0)
    amounts = jnp.concatenate(
        [
            orbit_shift,
            jnp.broadcast_to((orbit_shift[0] + bottom) % total, (7,)),
            ((orbit_shift[height - 1] + top) % total)[None],
        ]
    )
    shift = jnp.broadcast_to(amounts[:, None], (height + 8, LANES))
    f32 = jnp.float32

    def shaped(*shape):
        return jax.ShapeDtypeStruct(shape, f32)

    vmem = pl.BlockSpec(memory_space=pltpu.VMEM)
    dma = pltpu.SemaphoreType.DMA
    moved = pl.pallas_call(
        functools.partial(move_kernel, count, rads),
        out_shape=[
            shaped(fields, planes, height, LANES),
            shaped(count, 8, LANES),
            shaped(2, count, per, LANES),
            shaped(2, count, 8, LANES),
            shaped(2, fields, height, LANES),
            shaped(count, 8, LANES),
            shaped(2, count, per, LANES),
            shaped(2, count, 8, LANES),
        ],
        in_specs=[vmem] * 2,
        out_specs=[vmem] * 8,
        scratch_shapes=[
            pltpu.VMEM((count, per, height, LANES), f32),
            pltpu.VMEM((count, per, height, LANES), f32),
            pltpu.VMEM((count, 8, LANES), f32),
            pltpu.VMEM((count, 2, per, LANES), f32),
            dma((per, count)),
            dma((per, count)),
            dma((per, count)),
            dma((per, count)),
            dma((5 * count,)),
            dma((5 * count,)),
            dma((5,)),
            dma((5,)),
            dma((1,)),
        ],
        compiler_params=pltpu.CompilerParams(
            collective_id=0, has_side_effects=True, vmem_limit_bytes=24 * 1024 * 1024
        ),
        name="move",
    )(state.reshape(fields * planes, height, width), shift)
    tall = height + 8
    return pl.pallas_call(
        functools.partial(step_kernel, count),
        out_shape=shaped(*state.shape),
        in_specs=[vmem] * 8,
        out_specs=vmem,
        scratch_shapes=[
            pltpu.VMEM((planes + 2, fields, tall, LANES), f32),
            pltpu.VMEM((fields, tall, LANES), f32),
            pltpu.VMEM((fields, tall, LANES), f32),
            pltpu.VMEM((planes + 2, tall, LANES), f32),
            pltpu.VMEM((planes + 2, tall, LANES), f32),
            pltpu.VMEM((planes + 2, tall, LANES), f32),
            pltpu.VMEM((planes + 2, 5, height, LANES), f32),
            pltpu.VMEM((planes + 2, 2, height, LANES), f32),
            pltpu.VMEM((planes + 1, 8, height, LANES), f32),
            pltpu.VMEM((8, tall, LANES), f32),
            pltpu.VMEM((tall, LANES), f32),
            pltpu.VMEM((tall, LANES), f32),
        ],
        compiler_params=pltpu.CompilerParams(vmem_limit_bytes=24 * 1024 * 1024),
        name="step",
    )(*moved)


def solution(mesh):
    return jax.shard_map(
        per_device,
        mesh=mesh,
        in_specs=(P("groups", "vert", "rad", "az"), P(("groups", "rad")), P("groups")),
        out_specs=P("groups", "vert", "rad", "az"),
        check_vma=False,
    )
```

```python
import functools

import jax
import jax.numpy as jnp
from jax import lax
from jax.experimental import pallas as pl
from jax.experimental.pallas import tpu as pltpu
from jax.sharding import PartitionSpec as P

ADIABATIC = 5.0 / 3.0
TIME_STEP = 0.125
ROTATION = 1.0
SHEAR_RATE = 1.5
MESH = pl.DeviceIdType.MESH
LANES = 128


def lane_index(shape):
    return lax.broadcasted_iota(jnp.int32, shape, len(shape) - 1)


def halves_of(per, planes):
    return 2 if per % planes == 0 and planes == 4 else 1


def pair_of_step(step, per, planes):
    if halves_of(per, planes) == 2:
        fields = per // planes
        return (step % fields) * planes + (3 * (step // fields)) % planes
    return step


def place_of_pair(pair, per, planes):
    held = per // halves_of(per, planes)
    steps = {pair_of_step(step, per, planes): step for step in range(per)}
    return divmod(steps[pair], held)


def move_kernel(
    count,
    rads,
    orbit,
    remap,
    state,
    main,
    ghost_cols,
    ghost_rows,
    side_cols,
    z_main,
    z_cols,
    z_rows,
    z_side,
    rows,
    turned,
    shift,
    out_cols,
    out_rows,
    send1,
    recv1,
    send2,
    recv2,
    send3,
    recv3,
    send4,
    recv4,
    own_sem,
):
    fields, planes, height, _ = main.shape
    per = fields * planes // count
    halves = halves_of(per, planes)
    held = per // halves
    sides = side_cols.shape[0]
    total = count * LANES
    tiles = height // 8
    group = lax.axis_index("groups")
    me = lax.axis_index("az")
    rad = lax.axis_index("rad")
    core = lax.axis_index("vert")
    up = (rad + 1) % rads
    down = (rad + rads - 1) % rads

    def device(az, r, v):
        return (group, az, r, v)

    barrier = pltpu.get_barrier_semaphore()
    targets = [device((me + d) % count, rad, core) for d in range(1, count)]
    for d in range(count):
        targets.append(device((me + d) % count, up, core))
        if sides > 1:
            targets.append(device((me + d) % count, down, core))
    targets.append(device(me, rad, 1 - core))
    for target in targets:
        pl.semaphore_signal(barrier, inc=1, device_id=target, device_id_type=MESH)

    own = pltpu.make_async_copy(state.at[pl.ds(me * per, per)], rows.at[me], own_sem.at[0])
    own.start()
    lane8 = lane_index((8, LANES))
    sub8 = lax.broadcasted_iota(jnp.int32, (8, LANES), 0)
    for t in range(tiles):
        amount = jnp.full((8, LANES), orbit[8 * t], jnp.int32)
        for i in range(1, 8):
            amount = jnp.where(sub8 == i, orbit[8 * t + i], amount)
        shift[pl.ds(8 * t, 8), :] = amount
    top = orbit[height - 1] + jnp.where(rad == rads - 1, remap[0], 0)
    bottom = orbit[0] + jnp.where(rad == 0, total - remap[0], 0)
    amount = jnp.where(sub8 == 7, top, bottom)
    shift[pl.ds(height, 8), :] = jnp.where(amount >= total, amount - total, amount)
    out_cols[...] = jnp.zeros_like(out_cols)
    pl.semaphore_wait(barrier, len(targets))

    def first(step, d):
        pair = pair_of_step(step, per, planes)
        peer = (me + d) % count
        return pltpu.make_async_remote_copy(
            src_ref=state.at[peer * per + pair],
            dst_ref=rows.at[me, pair],
            send_sem=send1.at[step, d],
            recv_sem=recv1.at[step, d],
            device_id=device(peer, rad, core),
            device_id_type=MESH,
        )

    def second(step, d):
        pair = pair_of_step(step, per, planes)
        peer = (me + d) % count
        whole = me * per + pair
        return pltpu.make_async_remote_copy(
            src_ref=turned.at[peer, pair],
            dst_ref=main.at[whole // planes, whole % planes],
            send_sem=send2.at[step, d],
            recv_sem=recv2.at[step, d],
            device_id=device(peer, rad, core),
            device_id_type=MESH,
        )

    def ghosts(half):
        copies = []
        base = half * 5 * count

        def add(source, target, slot, d, r):
            copies.append(
                pltpu.make_async_remote_copy(
                    src_ref=source,
                    dst_ref=target,
                    send_sem=send3.at[base + slot],
                    recv_sem=recv3.at[base + slot],
                    device_id=device((me + d) % count, r, core),
                    device_id_type=MESH,
                )
            )

        for d in range(count):
            peer = (me + d) % count
            if d > 0:
                add(out_cols.at[half, peer], ghost_cols.at[half, me], d, d, rad)
            for side in range(sides):
                r = up if side == sides - 1 else down
                slot = count + d * 4 + side * 2
                add(out_rows.at[half, peer], ghost_rows.at[side, half, me], slot, d, r)
                add(out_cols.at[half, peer], side_cols.at[side, half, me], slot + 1, d, r)
        return copies

    def start_first(step, carry):
        for d in range(1, count):
            first(step, d).start()
        return carry

    lax.fori_loop(0, per, start_first, 0)
    own.wait()
    bits = [bit for bit in range(31) if (1 << bit) < total]

    def turn(step, half):
        pair = pair_of_step(step, per, planes)
        slot = step - half * held
        for d in range(1, count):
            first(step, d).wait_recv()
        for t in range(tiles + 1):
            amount = shift[pl.ds(8 * t, 8), :]
            if t < tiles:
                blocks = [rows[b, pair, pl.ds(8 * t, 8), :] for b in range(count)]
            else:
                blocks = [
                    jnp.where(
                        sub8 == 7,
                        rows[b, pair, pl.ds(height - 1, 1), :],
                        rows[b, pair, pl.ds(0, 1), :],
                    )
                    for b in range(count)
                ]
            for bit in bits:
                if (1 << bit) < LANES:
                    continue
                q = (1 << bit) // LANES
                flag = ((amount >> bit) & 1) == 1
                blocks = [
                    jnp.where(flag, blocks[(b - q) % count], blocks[b]) for b in range(count)
                ]
            for bit in bits:
                if (1 << bit) >= LANES:
                    continue
                flag = ((amount >> bit) & 1) == 1
                blocks = [
                    jnp.where(flag, pltpu.roll(block, 1 << bit, 1), block) for block in blocks
                ]
            inside = lane8 >= (amount & (LANES - 1))
            out = [
                jnp.where(inside, blocks[b], blocks[(b - 1) % count]) for b in range(count)
            ]
            place = 2 * held * t + 2 * slot
            for b in range(count):
                low = jnp.broadcast_to(out[(b - 1) % count][:, LANES - 1 :], (8, LANES))
                high = jnp.broadcast_to(out[(b + 1) % count][:, :1], (8, LANES))
                out_cols[half, b] = jnp.where(
                    lane8 == place, low, jnp.where(lane8 == place + 1, high, out_cols[half, b])
                )
                if t < tiles:
                    turned[b, pair, pl.ds(8 * t, 8), :] = out[b]
                else:
                    out_rows[half, b, pl.ds(slot, 1), :] = out[b][0:1]
                    out_rows[half, b, pl.ds(held + slot, 1), :] = out[b][7:8]
        for d in range(1, count):
            second(step, d).start()
        whole = me * per + pair
        main[whole // planes, whole % planes] = turned[me, pair]

    small = []
    for half in range(halves):

        def body(step, carry, half=half):
            turn(step, half)
            return carry

        lax.fori_loop(half * held, (half + 1) * held, body, 0)
        small.append(ghosts(half))
        for copy in small[half]:
            copy.start()
        ghost_cols[half, me] = out_cols[half, me]

    def wait_second(step, carry):
        for d in range(1, count):
            second(step, d).wait_recv()
        return carry

    def across(index, source, target):
        return pltpu.make_async_remote_copy(
            src_ref=source,
            dst_ref=target,
            send_sem=send4.at[index],
            recv_sem=recv4.at[index],
            device_id=device(me, rad, 1 - core),
            device_id_type=MESH,
        )

    lax.fori_loop(0, held, wait_second, 0)
    for copy in small[0]:
        copy.wait_recv()
    last = [
        across(0, main.at[:, planes - 1], z_main.at[0]),
        across(1, main.at[:, 0], z_main.at[1]),
        across(2, ghost_cols.at[0], z_cols),
    ]
    for side in range(sides):
        last.append(across(3 + 2 * side, ghost_rows.at[side, 0], z_rows.at[side]))
        last.append(across(4 + 2 * side, side_cols.at[side, 0], z_side.at[side]))
    for copy in last:
        copy.start()
    for half in range(1, halves):
        lax.fori_loop(half * held, (half + 1) * held, wait_second, 0)
        for copy in small[half]:
            copy.wait_recv()
    for copy in last:
        copy.wait()

    def finish(step, carry):
        for d in range(1, count):
            first(step, d).wait_send()
            second(step, d).wait_send()
        return carry

    lax.fori_loop(0, per, finish, 0)
    for half in range(halves):
        for copy in small[half]:
            copy.wait_send()


def primitives(cells):
    density, mx, my, mz, energy, bx, by, bz = cells
    inverse = 1.0 / density
    velocity = (mx * inverse, my * inverse, mz * inverse)
    magnet_sq = bx * bx + by * by + bz * bz
    kinetic = 0.5 * (mx * velocity[0] + my * velocity[1] + mz * velocity[2])
    pressure = (ADIABATIC - 1.0) * (energy - kinetic - 0.5 * magnet_sq)
    total_pressure = pressure + 0.5 * magnet_sq
    projection = velocity[0] * bx + velocity[1] * by + velocity[2] * bz
    fast_speed = jnp.sqrt((ADIABATIC * pressure + magnet_sq) * inverse)
    return velocity, total_pressure, projection, fast_speed


def one_flux(cells, prims, normal, piece):
    velocity, total_pressure, projection, _ = prims
    speed = velocity[normal]
    field = cells[5 + normal]
    if piece == 0:
        return cells[1 + normal]
    if piece < 4:
        value = cells[piece] * speed - cells[piece + 4] * field
        return value + total_pressure if piece == normal + 1 else value
    if piece == 4:
        return (cells[4] + total_pressure) * speed - field * projection
    return cells[piece] * speed - velocity[piece - 5] * field


def face_flux(left, left_prims, right, right_prims, normal, pieces):
    ls, lc = left_prims[0][normal], left_prims[3]
    rs, rc = right_prims[0][normal], right_prims[3]
    low = jnp.minimum(jnp.minimum(ls - lc, rs - rc), 0.0)
    high = jnp.maximum(jnp.maximum(ls + lc, rs + rc), 0.0)
    inverse = 1.0 / (high - low)
    wl = high * inverse
    wr = low * inverse
    wd = low * wl
    out = []
    for piece in pieces:
        if piece == 5 + normal:
            out.append(wd * (right[piece] - left[piece]))
            continue
        out.append(
            wl * one_flux(left, left_prims, normal, piece)
            - wr * one_flux(right, right_prims, normal, piece)
            + wd * (right[piece] - left[piece])
        )
    return out


def step_kernel(
    count,
    main,
    ghost_cols,
    ghost_rows,
    side_cols,
    z_main,
    z_cols,
    z_rows,
    z_side,
    result,
    new,
    sems,
    pad,
    cols,
    edge,
    fx7,
    fy7,
    fyr7,
    change,
    curl,
    zface,
    gy,
    gx6,
    gz6,
):
    fields, planes, height, _ = main.shape
    per = fields * planes // count
    tiles = height // 8
    tall = height + 8
    lane8 = lane_index((8, LANES))
    sub8 = lax.broadcasted_iota(jnp.int32, (8, LANES), 0)
    lane = lane_index((tall, LANES))
    padded = planes + 2

    sides = side_cols.shape[0]
    held = per // halves_of(per, planes)

    def source_of(f, p):
        k = (p - 1) % planes
        owner, pair = divmod(f * planes + k, per)
        half, slot = place_of_pair(pair, per, planes)
        return k, owner, half, slot

    for f in range(fields):
        for p in range(padded):
            k, owner, half, slot = source_of(f, p)
            low, high = pl.ds(slot, 1), pl.ds(held + slot, 1)
            if 1 <= p <= planes:
                pad[p, f, pl.ds(0, height)] = main[f, k]
                before = ghost_rows[sides - 1, half, owner, high, :]
                after = ghost_rows[0, half, owner, low, :]
            else:
                pad[p, f, pl.ds(0, height)] = z_main[0 if p == 0 else 1, f]
                before = z_rows[sides - 1, owner, high, :]
                after = z_rows[0, owner, low, :]
            pad[p, f, pl.ds(height, 8)] = jnp.where(sub8 == 7, before, after)
        for t in range(tiles + 1):
            tile = jnp.ones((8, LANES), jnp.float32)
            for p in range(padded):
                k, owner, half, slot = source_of(f, p)
                inner = 1 <= p <= planes
                if t < tiles:
                    source = ghost_cols[half, owner] if inner else z_cols[owner]
                elif inner:
                    source = jnp.where(
                        sub8 == 7, side_cols[sides - 1, half, owner], side_cols[0, half, owner]
                    )
                else:
                    source = jnp.where(sub8 == 7, z_side[sides - 1, owner], z_side[0, owner])
                moved = pltpu.roll(source, (2 * p - 2 * held * t - 2 * slot) % LANES, 1)
                tile = jnp.where(lane8 // 2 == p, moved, tile)
            cols[f, pl.ds(8 * t, 8)] = tile
        tile = jnp.ones((tall, LANES), jnp.float32)
        for p in range(padded):
            tile = jnp.where(lane // 2 == p, pltpu.roll(pad[p, f], 2 * p + 2, 1), tile)
        edge[f] = tile

    def below(x):
        return pltpu.roll(x, 1, 0)

    def above(x):
        return pltpu.roll(x, tall - 1, 0)

    ghost = [cols[f] for f in range(fields)]
    ghost_prims = primitives(ghost)
    last = [edge[f] for f in range(fields)]
    for piece, value in enumerate(
        face_flux(last, primitives(last), ghost, ghost_prims, 1, range(8))
    ):
        gy[piece] = value
    lower = [below(x) for x in ghost]
    gx6[...] = face_flux(lower, primitives(lower), ghost, ghost_prims, 0, (6,))[0]
    higher = [pltpu.roll(x, LANES - 2, 1) for x in ghost]
    gz6[...] = face_flux(ghost, ghost_prims, higher, primitives(higher), 2, (6,))[0]

    def left_of(x, ghosts, p):
        return jnp.where(lane == 0, pltpu.roll(ghosts, LANES - 2 * p, 1), pltpu.roll(x, 1, 1))

    def right_of(x, ghosts, p):
        return jnp.where(
            lane == LANES - 1,
            pltpu.roll(ghosts, LANES - 2 - 2 * p, 1),
            pltpu.roll(x, LANES - 1, 1),
        )

    def in_plane(p, carry):
        cells = [pad[p, f] for f in range(fields)]
        prims = primitives(cells)
        lower = [below(x) for x in cells]
        flux = face_flux(lower, primitives(lower), cells, prims, 0, range(8))
        fx7[p] = flux[7]
        for f in range(5):
            change[p, f] = (above(flux[f]) - flux[f])[:height]
        x6 = flux[6]
        side = [left_of(cells[f], cols[f], p) for f in range(fields)]
        flux = face_flux(side, primitives(side), cells, prims, 1, range(8))
        fy7[p] = flux[7]
        fyr7[p] = right_of(flux[7], gy[7], p)
        for f in range(5):
            change[p, f] += (right_of(flux[f], gy[f], p) - flux[f])[:height]
        y5 = flux[5]
        y5r = right_of(y5, gy[5], p)
        x6l = left_of(x6, gx6[...], p)
        x6r = right_of(x6, gx6[...], p)
        ez = 0.25 * (y5 + below(y5) - (x6 + x6l))
        ezr = 0.25 * (y5r + below(y5r) - (x6r + x6))
        ez_up = above(ez)
        ezr_up = above(ezr)
        curl[p, 0] = (0.5 * ((ezr_up + ezr) - (ez_up + ez)))[:height]
        curl[p, 1] = (0.5 * ((ezr_up + ez_up) - (ezr + ez)))[:height]
        return carry

    lax.fori_loop(0, padded, in_plane, 0)

    def between(q, carry):
        low = [pad[q, f] for f in range(fields)]
        high = [pad[q + 1, f] for f in range(fields)]
        flux = face_flux(low, primitives(low), high, primitives(high), 2, range(8))
        for f in range(5):
            zface[q, f] = flux[f][:height]
        z5, z6 = flux[5], flux[6]
        ey = 0.25 * (fx7[q + 1] + fx7[q] - (z5 + below(z5)))
        ex = 0.25 * (z6 + left_of(z6, gz6[...], q) - (fy7[q + 1] + fy7[q]))
        exr = 0.25 * (right_of(z6, gz6[...], q) + z6 - (fyr7[q + 1] + fyr7[q]))
        ey_up = above(ey)
        zface[q, 5] = (0.5 * (ey_up + ey))[:height]
        zface[q, 6] = (0.5 * (exr + ex))[:height]
        zface[q, 7] = (0.5 * ((ey_up - ey) - (exr - ex)))[:height]
        return carry

    lax.fori_loop(0, planes + 1, between, 0)

    def combine(k, carry):
        p = k + 1
        old = [pad[p, f, pl.ds(0, height)] for f in range(fields)]
        hydro = [
            old[f] - TIME_STEP * (change[p, f] + (zface[p, f] - zface[k, f])) for f in range(5)
        ]
        new[0, k] = hydro[0]
        new[1, k] = hydro[1] + TIME_STEP * 2.0 * ROTATION * old[2]
        new[2, k] = hydro[2] + TIME_STEP * (SHEAR_RATE - 2.0) * ROTATION * old[1]
        new[3, k] = hydro[3]
        new[4, k] = hydro[4]
        new[5, k] = old[5] - TIME_STEP * (curl[p, 0] - (zface[p, 5] - zface[k, 5]))
        new[6, k] = old[6] - TIME_STEP * ((zface[p, 6] - zface[k, 6]) - curl[p, 1])
        new[7, k] = old[7] - TIME_STEP * (zface[p, 7] + zface[k, 7])
        store(k).start()
        return carry

    def store(k):
        return pltpu.make_async_copy(new.at[:, k], result.at[:, k], sems.at[k])

    lax.fori_loop(0, planes, combine, 0)
    for k in range(planes):
        store(k).wait()


def per_device(state, orbit_shift, remap_shift):
    count = lax.axis_size("az")
    rads = lax.axis_size("rad")
    fields, planes, height, width = state.shape
    per = fields * planes // count
    halves = halves_of(per, planes)
    held = per // halves
    sides = 1 if rads == 2 else 2
    f32 = jnp.float32

    def shaped(*shape):
        return jax.ShapeDtypeStruct(shape, f32)

    vmem = pl.BlockSpec(memory_space=pltpu.VMEM)
    smem = pl.BlockSpec(memory_space=pltpu.SMEM)
    anywhere = pl.BlockSpec(memory_space=pl.ANY)
    dma = pltpu.SemaphoreType.DMA
    moved = pl.pallas_call(
        functools.partial(move_kernel, count, rads),
        out_shape=[
            shaped(fields, planes, height, LANES),
            shaped(halves, count, 8, LANES),
            shaped(sides, halves, count, 2 * held, LANES),
            shaped(sides, halves, count, 8, LANES),
            shaped(2, fields, height, LANES),
            shaped(count, 8, LANES),
            shaped(sides, count, 2 * held, LANES),
            shaped(sides, count, 8, LANES),
        ],
        in_specs=[smem, smem, anywhere],
        out_specs=[vmem] * 8,
        scratch_shapes=[
            pltpu.VMEM((count, per, height, LANES), f32),
            pltpu.VMEM((count, per, height, LANES), f32),
            pltpu.VMEM((height + 8, LANES), jnp.int32),
            pltpu.VMEM((halves, count, 8, LANES), f32),
            pltpu.VMEM((halves, count, 2 * held, LANES), f32),
            dma((per, count)),
            dma((per, count)),
            dma((per, count)),
            dma((per, count)),
            dma((5 * count * halves,)),
            dma((5 * count * halves,)),
            dma((7,)),
            dma((7,)),
            dma((1,)),
        ],
        compiler_params=pltpu.CompilerParams(
            collective_id=0, has_side_effects=True, vmem_limit_bytes=24 * 1024 * 1024
        ),
        name="move",
    )(orbit_shift, remap_shift, state.reshape(fields * planes, height, width))
    tall = height + 8
    return pl.pallas_call(
        functools.partial(step_kernel, count),
        out_shape=shaped(*state.shape),
        in_specs=[vmem] * 8,
        out_specs=anywhere,
        scratch_shapes=[
            pltpu.VMEM(state.shape, f32),
            dma((planes,)),
            pltpu.VMEM((planes + 2, fields, tall, LANES), f32),
            pltpu.VMEM((fields, tall, LANES), f32),
            pltpu.VMEM((fields, tall, LANES), f32),
            pltpu.VMEM((planes + 2, tall, LANES), f32),
            pltpu.VMEM((planes + 2, tall, LANES), f32),
            pltpu.VMEM((planes + 2, tall, LANES), f32),
            pltpu.VMEM((planes + 2, 5, height, LANES), f32),
            pltpu.VMEM((planes + 2, 2, height, LANES), f32),
            pltpu.VMEM((planes + 1, 8, height, LANES), f32),
            pltpu.VMEM((8, tall, LANES), f32),
            pltpu.VMEM((tall, LANES), f32),
            pltpu.VMEM((tall, LANES), f32),
        ],
        compiler_params=pltpu.CompilerParams(vmem_limit_bytes=24 * 1024 * 1024),
        name="step",
    )(*moved)


def solution(mesh):
    return jax.shard_map(
        per_device,
        mesh=mesh,
        in_specs=(P("groups", "vert", "rad", "az"), P(("groups", "rad")), P("groups")),
        out_specs=P("groups", "vert", "rad", "az"),
        check_vma=False,
    )
```

```python
import functools

import jax
import jax.numpy as jnp
from jax import lax
from jax.experimental import pallas as pl
from jax.experimental.pallas import tpu as pltpu
from jax.sharding import PartitionSpec as P

ADIABATIC = 5.0 / 3.0
TIME_STEP = 0.125
ROTATION = 1.0
SHEAR_RATE = 1.5
MESH = pl.DeviceIdType.MESH
LANES = 128


def lane_index(shape):
    return lax.broadcasted_iota(jnp.int32, shape, len(shape) - 1)


def halves_of(per, planes):
    return 2 if per % planes == 0 and planes == 4 else 1


def pair_of_step(step, per, planes):
    if halves_of(per, planes) == 2:
        fields = per // planes
        return (step % fields) * planes + (3 * (step // fields)) % planes
    return step


def place_of_pair(pair, per, planes):
    held = per // halves_of(per, planes)
    steps = {pair_of_step(step, per, planes): step for step in range(per)}
    return divmod(steps[pair], held)


def move_kernel(
    count,
    rads,
    stages,
    orbit,
    remap,
    state,
    main,
    ghost_cols,
    ghost_rows,
    side_cols,
    z_main,
    z_cols,
    z_rows,
    z_side,
    rows,
    turned,
    shift,
    out_cols,
    out_rows,
    send1,
    recv1,
    send2,
    recv2,
    send3,
    recv3,
    send4,
    recv4,
    own_sem,
):
    fields, planes, height, _ = main.shape
    per = fields * planes // count
    halves = halves_of(per, planes)
    held = per // halves
    sides = side_cols.shape[0]
    total = count * LANES
    tiles = height // 8
    group = lax.axis_index("groups")
    me = lax.axis_index("az")
    rad = lax.axis_index("rad")
    core = lax.axis_index("vert")
    up = (rad + 1) % rads
    down = (rad + rads - 1) % rads

    def device(az, r, v):
        return (group, az, r, v)

    barrier = pltpu.get_barrier_semaphore()
    targets = [device((me + d) % count, rad, core) for d in range(1, count)]
    for d in range(count):
        targets.append(device((me + d) % count, up, core))
        if sides > 1:
            targets.append(device((me + d) % count, down, core))
    targets.append(device(me, rad, 1 - core))
    for target in targets:
        pl.semaphore_signal(barrier, inc=1, device_id=target, device_id_type=MESH)

    own = pltpu.make_async_copy(state.at[pl.ds(me * per, per)], rows.at[me], own_sem.at[0])
    own.start()
    lane8 = lane_index((8, LANES))
    sub8 = lax.broadcasted_iota(jnp.int32, (8, LANES), 0)
    for t in range(tiles):
        amount = jnp.full((8, LANES), orbit[8 * t], jnp.int32)
        for i in range(1, 8):
            amount = jnp.where(sub8 == i, orbit[8 * t + i], amount)
        shift[pl.ds(8 * t, 8), :] = amount
    top = orbit[height - 1] + jnp.where(rad == rads - 1, remap[0], 0)
    bottom = orbit[0] + jnp.where(rad == 0, total - remap[0], 0)
    amount = jnp.where(sub8 == 7, top, bottom)
    shift[pl.ds(height, 8), :] = jnp.where(amount >= total, amount - total, amount)
    out_cols[...] = jnp.zeros_like(out_cols)
    pl.semaphore_wait(barrier, len(targets))

    def first(step, d):
        pair = pair_of_step(step, per, planes)
        peer = (me + d) % count
        return pltpu.make_async_remote_copy(
            src_ref=state.at[peer * per + pair],
            dst_ref=rows.at[me, pair],
            send_sem=send1.at[step, d],
            recv_sem=recv1.at[step, d],
            device_id=device(peer, rad, core),
            device_id_type=MESH,
        )

    def second(step, d):
        pair = pair_of_step(step, per, planes)
        peer = (me + d) % count
        whole = me * per + pair
        return pltpu.make_async_remote_copy(
            src_ref=turned.at[peer, pair],
            dst_ref=main.at[whole // planes, whole % planes],
            send_sem=send2.at[step, d],
            recv_sem=recv2.at[step, d],
            device_id=device(peer, rad, core),
            device_id_type=MESH,
        )

    def ghosts(half):
        copies = []
        base = half * 5 * count

        def add(source, target, slot, d, r):
            copies.append(
                pltpu.make_async_remote_copy(
                    src_ref=source,
                    dst_ref=target,
                    send_sem=send3.at[base + slot],
                    recv_sem=recv3.at[base + slot],
                    device_id=device((me + d) % count, r, core),
                    device_id_type=MESH,
                )
            )

        for d in range(count):
            peer = (me + d) % count
            if d > 0:
                add(out_cols.at[half, peer], ghost_cols.at[half, me], d, d, rad)
            for side in range(sides):
                r = up if side == sides - 1 else down
                slot = count + d * 4 + side * 2
                add(out_rows.at[half, peer], ghost_rows.at[side, half, me], slot, d, r)
                add(out_cols.at[half, peer], side_cols.at[side, half, me], slot + 1, d, r)
        return copies

    def start_first(step, carry):
        for d in range(1, count):
            first(step, d).start()
        return carry

    lax.fori_loop(0, per, start_first, 0)
    own.wait()
    bits = [bit for bit in range(31) if (1 << bit) < total]

    def turn(step, half):
        pair = pair_of_step(step, per, planes)
        slot = step - half * held
        for d in range(1, count):
            first(step, d).wait_recv()
        for t in range(tiles + 1):
            amount = shift[pl.ds(8 * t, 8), :]
            if t < tiles:
                blocks = [rows[b, pair, pl.ds(8 * t, 8), :] for b in range(count)]
            else:
                blocks = [
                    jnp.where(
                        sub8 == 7,
                        rows[b, pair, pl.ds(height - 1, 1), :],
                        rows[b, pair, pl.ds(0, 1), :],
                    )
                    for b in range(count)
                ]
            for bit in bits:
                if (1 << bit) < LANES:
                    continue
                q = (1 << bit) // LANES
                flag = ((amount >> bit) & 1) == 1
                blocks = [
                    jnp.where(flag, blocks[(b - q) % count], blocks[b]) for b in range(count)
                ]
            for bit in bits:
                if (1 << bit) >= LANES:
                    continue
                flag = ((amount >> bit) & 1) == 1
                blocks = [
                    jnp.where(flag, pltpu.roll(block, 1 << bit, 1), block) for block in blocks
                ]
            inside = lane8 >= (amount & (LANES - 1))
            out = [
                jnp.where(inside, blocks[b], blocks[(b - 1) % count]) for b in range(count)
            ]
            place = 2 * held * t + 2 * slot
            for b in range(count):
                low = jnp.broadcast_to(out[(b - 1) % count][:, LANES - 1 :], (8, LANES))
                high = jnp.broadcast_to(out[(b + 1) % count][:, :1], (8, LANES))
                out_cols[half, b] = jnp.where(
                    lane8 == place, low, jnp.where(lane8 == place + 1, high, out_cols[half, b])
                )
                if t < tiles:
                    turned[b, pair, pl.ds(8 * t, 8), :] = out[b]
                else:
                    out_rows[half, b, pl.ds(slot, 1), :] = out[b][0:1]
                    out_rows[half, b, pl.ds(held + slot, 1), :] = out[b][7:8]
        for d in range(1, count):
            second(step, d).start()
        whole = me * per + pair
        main[whole // planes, whole % planes] = turned[me, pair]

    small = []
    for half in range(halves):

        def body(step, carry, half=half):
            turn(step, half)
            return carry

        lax.fori_loop(half * held, (half + 1) * held, body, 0)
        small.append(ghosts(half))
        for copy in small[half]:
            copy.start()
        ghost_cols[half, me] = out_cols[half, me]

    def wait_second(step, carry):
        for d in range(1, count):
            second(step, d).wait_recv()
        return carry

    def across(index, source, target):
        return pltpu.make_async_remote_copy(
            src_ref=source,
            dst_ref=target,
            send_sem=send4.at[index],
            recv_sem=recv4.at[index],
            device_id=device(me, rad, 1 - core),
            device_id_type=MESH,
        )

    lax.fori_loop(0, held, wait_second, 0)
    for copy in small[0]:
        copy.wait_recv()
    last = [
        across(0, main.at[:, planes - 1], z_main.at[0]),
        across(1, main.at[:, 0], z_main.at[1]),
        across(2, ghost_cols.at[0], z_cols),
    ]
    for side in range(sides):
        last.append(across(3 + 2 * side, ghost_rows.at[side, 0], z_rows.at[side]))
        last.append(across(4 + 2 * side, side_cols.at[side, 0], z_side.at[side]))
    for copy in last:
        copy.start()
    stages[0]()
    for copy in last:
        copy.wait_recv()
    stages[1]()
    for half in range(1, halves):
        lax.fori_loop(half * held, (half + 1) * held, wait_second, 0)
        for copy in small[half]:
            copy.wait_recv()
    stages[2]()
    for copy in last:
        copy.wait_send()

    def finish(step, carry):
        for d in range(1, count):
            first(step, d).wait_send()
            second(step, d).wait_send()
        return carry

    lax.fori_loop(0, per, finish, 0)
    for half in range(halves):
        for copy in small[half]:
            copy.wait_send()


def primitives(cells):
    density, mx, my, mz, energy, bx, by, bz = cells
    inverse = 1.0 / density
    velocity = (mx * inverse, my * inverse, mz * inverse)
    magnet_sq = bx * bx + by * by + bz * bz
    kinetic = 0.5 * (mx * velocity[0] + my * velocity[1] + mz * velocity[2])
    pressure = (ADIABATIC - 1.0) * (energy - kinetic - 0.5 * magnet_sq)
    total_pressure = pressure + 0.5 * magnet_sq
    projection = velocity[0] * bx + velocity[1] * by + velocity[2] * bz
    fast_speed = jnp.sqrt((ADIABATIC * pressure + magnet_sq) * inverse)
    return velocity, total_pressure, projection, fast_speed


def one_flux(cells, prims, normal, piece):
    velocity, total_pressure, projection, _ = prims
    speed = velocity[normal]
    field = cells[5 + normal]
    if piece == 0:
        return cells[1 + normal]
    if piece < 4:
        value = cells[piece] * speed - cells[piece + 4] * field
        return value + total_pressure if piece == normal + 1 else value
    if piece == 4:
        return (cells[4] + total_pressure) * speed - field * projection
    return cells[piece] * speed - velocity[piece - 5] * field


def face_flux(left, left_prims, right, right_prims, normal, pieces):
    ls, lc = left_prims[0][normal], left_prims[3]
    rs, rc = right_prims[0][normal], right_prims[3]
    low = jnp.minimum(jnp.minimum(ls - lc, rs - rc), 0.0)
    high = jnp.maximum(jnp.maximum(ls + lc, rs + rc), 0.0)
    inverse = 1.0 / (high - low)
    wl = high * inverse
    wr = low * inverse
    wd = low * wl
    out = []
    for piece in pieces:
        if piece == 5 + normal:
            out.append(wd * (right[piece] - left[piece]))
            continue
        out.append(
            wl * one_flux(left, left_prims, normal, piece)
            - wr * one_flux(right, right_prims, normal, piece)
            + wd * (right[piece] - left[piece])
        )
    return out


def step_stages(
    count,
    main,
    ghost_cols,
    ghost_rows,
    side_cols,
    z_main,
    z_cols,
    z_rows,
    z_side,
    new,
    pad,
    cols,
    edge,
    fx7,
    fy7,
    fyr7,
    change,
    curl,
    zface,
    gy,
    gx6,
    gz6,
):
    fields, planes, height, _ = main.shape
    per = fields * planes // count
    tiles = height // 8
    tall = height + 8
    lane8 = lane_index((8, LANES))
    sub8 = lax.broadcasted_iota(jnp.int32, (8, LANES), 0)
    lane = lane_index((tall, LANES))
    padded = planes + 2

    sides = side_cols.shape[0]
    held = per // halves_of(per, planes)

    def source_of(f, p):
        k = (p - 1) % planes
        owner, pair = divmod(f * planes + k, per)
        half, slot = place_of_pair(pair, per, planes)
        return k, owner, half, slot

    def below(x):
        return pltpu.roll(x, 1, 0)

    def above(x):
        return pltpu.roll(x, tall - 1, 0)

    def assemble(chosen, fresh):
        for f in range(fields):
            for p in chosen:
                k, owner, half, slot = source_of(f, p)
                low, high = pl.ds(slot, 1), pl.ds(held + slot, 1)
                if 1 <= p <= planes:
                    pad[p, f, pl.ds(0, height)] = main[f, k]
                    before = ghost_rows[sides - 1, half, owner, high, :]
                    after = ghost_rows[0, half, owner, low, :]
                else:
                    pad[p, f, pl.ds(0, height)] = z_main[0 if p == 0 else 1, f]
                    before = z_rows[sides - 1, owner, high, :]
                    after = z_rows[0, owner, low, :]
                pad[p, f, pl.ds(height, 8)] = jnp.where(sub8 == 7, before, after)
            for t in range(tiles + 1):
                tile = jnp.zeros((8, LANES), jnp.float32) if fresh else cols[f, pl.ds(8 * t, 8)]
                for p in chosen:
                    k, owner, half, slot = source_of(f, p)
                    inner = 1 <= p <= planes
                    if t < tiles:
                        source = ghost_cols[half, owner] if inner else z_cols[owner]
                    elif inner:
                        source = jnp.where(
                            sub8 == 7, side_cols[sides - 1, half, owner], side_cols[0, half, owner]
                        )
                    else:
                        source = jnp.where(sub8 == 7, z_side[sides - 1, owner], z_side[0, owner])
                    moved = pltpu.roll(source, (2 * p - 2 * held * t - 2 * slot) % LANES, 1)
                    tile = jnp.where(lane8 // 2 == p, moved, tile)
                cols[f, pl.ds(8 * t, 8)] = tile
            tile = jnp.zeros((tall, LANES), jnp.float32) if fresh else edge[f]
            for p in chosen:
                tile = jnp.where(lane // 2 == p, pltpu.roll(pad[p, f], 2 * p + 2, 1), tile)
            edge[f] = tile

        ghost = [cols[f] for f in range(fields)]
        ghost_prims = primitives(ghost)
        last = [edge[f] for f in range(fields)]
        for piece, value in enumerate(
            face_flux(last, primitives(last), ghost, ghost_prims, 1, range(8))
        ):
            gy[piece] = value
        lower = [below(x) for x in ghost]
        gx6[...] = face_flux(lower, primitives(lower), ghost, ghost_prims, 0, (6,))[0]
        higher = [pltpu.roll(x, LANES - 2, 1) for x in ghost]
        gz6[...] = face_flux(ghost, ghost_prims, higher, primitives(higher), 2, (6,))[0]

    def left_of(x, ghosts, p):
        return jnp.where(lane == 0, pltpu.roll(ghosts, LANES - 2 * p, 1), pltpu.roll(x, 1, 1))

    def right_of(x, ghosts, p):
        return jnp.where(
            lane == LANES - 1,
            pltpu.roll(ghosts, LANES - 2 - 2 * p, 1),
            pltpu.roll(x, LANES - 1, 1),
        )

    def in_plane(p, carry):
        cells = [pad[p, f] for f in range(fields)]
        prims = primitives(cells)
        lower = [below(x) for x in cells]
        flux = face_flux(lower, primitives(lower), cells, prims, 0, range(8))
        fx7[p] = flux[7]
        for f in range(5):
            change[p, f] = (above(flux[f]) - flux[f])[:height]
        x6 = flux[6]
        side = [left_of(cells[f], cols[f], p) for f in range(fields)]
        flux = face_flux(side, primitives(side), cells, prims, 1, range(8))
        fy7[p] = flux[7]
        fyr7[p] = right_of(flux[7], gy[7], p)
        for f in range(5):
            change[p, f] += (right_of(flux[f], gy[f], p) - flux[f])[:height]
        y5 = flux[5]
        y5r = right_of(y5, gy[5], p)
        x6l = left_of(x6, gx6[...], p)
        x6r = right_of(x6, gx6[...], p)
        ez = 0.25 * (y5 + below(y5) - (x6 + x6l))
        ezr = 0.25 * (y5r + below(y5r) - (x6r + x6))
        ez_up = above(ez)
        ezr_up = above(ezr)
        curl[p, 0] = (0.5 * ((ezr_up + ezr) - (ez_up + ez)))[:height]
        curl[p, 1] = (0.5 * ((ezr_up + ez_up) - (ezr + ez)))[:height]
        return carry

    def between(q, carry):
        low = [pad[q, f] for f in range(fields)]
        high = [pad[q + 1, f] for f in range(fields)]
        flux = face_flux(low, primitives(low), high, primitives(high), 2, range(8))
        for f in range(5):
            zface[q, f] = flux[f][:height]
        z5, z6 = flux[5], flux[6]
        ey = 0.25 * (fx7[q + 1] + fx7[q] - (z5 + below(z5)))
        ex = 0.25 * (z6 + left_of(z6, gz6[...], q) - (fy7[q + 1] + fy7[q]))
        exr = 0.25 * (right_of(z6, gz6[...], q) + z6 - (fyr7[q + 1] + fyr7[q]))
        ey_up = above(ey)
        zface[q, 5] = (0.5 * (ey_up + ey))[:height]
        zface[q, 6] = (0.5 * (exr + ex))[:height]
        zface[q, 7] = (0.5 * ((ey_up - ey) - (exr - ex)))[:height]
        return carry

    def combine(k, carry):
        p = k + 1
        old = [pad[p, f, pl.ds(0, height)] for f in range(fields)]
        hydro = [
            old[f] - TIME_STEP * (change[p, f] + (zface[p, f] - zface[k, f])) for f in range(5)
        ]
        new[0, k] = hydro[0]
        new[1, k] = hydro[1] + TIME_STEP * 2.0 * ROTATION * old[2]
        new[2, k] = hydro[2] + TIME_STEP * (SHEAR_RATE - 2.0) * ROTATION * old[1]
        new[3, k] = hydro[3]
        new[4, k] = hydro[4]
        new[5, k] = old[5] - TIME_STEP * (curl[p, 0] - (zface[p, 5] - zface[k, 5]))
        new[6, k] = old[6] - TIME_STEP * ((zface[p, 6] - zface[k, 6]) - curl[p, 1])
        new[7, k] = old[7] - TIME_STEP * (zface[p, 7] + zface[k, 7])
        return carry

    def run(body, first, stride, times):
        lax.fori_loop(0, times, lambda i, carry: body(first + stride * i, carry), 0)

    early = halves_of(per, planes) == 2

    def outer():
        if early:
            assemble((1, planes), True)
            run(in_plane, 1, planes - 1, 2)

    def other_core():
        assemble((0, planes + 1), not early)
        run(in_plane, 0, planes + 1, 2)
        if early:
            run(between, 0, planes, 2)

    def inner():
        if early:
            assemble(tuple(range(2, planes)), False)
            run(in_plane, 2, 1, planes - 2)
            run(between, 1, 1, planes - 1)
        else:
            assemble(tuple(range(1, planes + 1)), False)
            run(in_plane, 1, 1, planes)
            run(between, 0, 1, planes + 1)
        run(combine, 0, 1, planes)

    return outer, other_core, inner


def whole_kernel(count, rads, orbit, remap, state, new, *scratch):
    landed, rest, work = scratch[:8], scratch[8:22], scratch[22:]
    stages = step_stages(count, *landed, new, *work)
    move_kernel(count, rads, stages, orbit, remap, state, *landed, *rest)


def per_device(state, orbit_shift, remap_shift):
    count = lax.axis_size("az")
    rads = lax.axis_size("rad")
    fields, planes, height, width = state.shape
    per = fields * planes // count
    halves = halves_of(per, planes)
    held = per // halves
    sides = 1 if rads == 2 else 2
    f32 = jnp.float32

    dma = pltpu.SemaphoreType.DMA
    tall = height + 8

    def held_in(*shape):
        return pltpu.VMEM(shape, f32)

    return pl.pallas_call(
        functools.partial(whole_kernel, count, rads),
        out_shape=jax.ShapeDtypeStruct(state.shape, f32),
        in_specs=[
            pl.BlockSpec(memory_space=pltpu.SMEM),
            pl.BlockSpec(memory_space=pltpu.SMEM),
            pl.BlockSpec(memory_space=pl.ANY),
        ],
        out_specs=pl.BlockSpec(memory_space=pltpu.VMEM),
        scratch_shapes=[
            held_in(fields, planes, height, LANES),
            held_in(halves, count, 8, LANES),
            held_in(sides, halves, count, 2 * held, LANES),
            held_in(sides, halves, count, 8, LANES),
            held_in(2, fields, height, LANES),
            held_in(count, 8, LANES),
            held_in(sides, count, 2 * held, LANES),
            held_in(sides, count, 8, LANES),
            held_in(count, per, height, LANES),
            held_in(count, per, height, LANES),
            pltpu.VMEM((tall, LANES), jnp.int32),
            held_in(halves, count, 8, LANES),
            held_in(halves, count, 2 * held, LANES),
            dma((per, count)),
            dma((per, count)),
            dma((per, count)),
            dma((per, count)),
            dma((5 * count * halves,)),
            dma((5 * count * halves,)),
            dma((7,)),
            dma((7,)),
            dma((1,)),
            held_in(planes + 2, fields, tall, LANES),
            held_in(fields, tall, LANES),
            held_in(fields, tall, LANES),
            held_in(planes + 2, tall, LANES),
            held_in(planes + 2, tall, LANES),
            held_in(planes + 2, tall, LANES),
            held_in(planes + 2, 5, height, LANES),
            held_in(planes + 2, 2, height, LANES),
            held_in(planes + 1, 8, height, LANES),
            held_in(8, tall, LANES),
            held_in(tall, LANES),
            held_in(tall, LANES),
        ],
        compiler_params=pltpu.CompilerParams(
            collective_id=0, has_side_effects=True, vmem_limit_bytes=24 * 1024 * 1024
        ),
        name="whole",
    )(orbit_shift, remap_shift, state.reshape(fields * planes, height, width))


def solution(mesh):
    return jax.shard_map(
        per_device,
        mesh=mesh,
        in_specs=(P("groups", "vert", "rad", "az"), P(("groups", "rad")), P("groups")),
        out_specs=P("groups", "vert", "rad", "az"),
        check_vma=False,
    )
```

```python
import functools

import jax
import jax.numpy as jnp
from jax import lax
from jax.experimental import pallas as pl
from jax.experimental.pallas import tpu as pltpu
from jax.sharding import PartitionSpec as P

ADIABATIC = 5.0 / 3.0
TIME_STEP = 0.125
ROTATION = 1.0
SHEAR_RATE = 1.5
MESH = pl.DeviceIdType.MESH
LANES = 128


def lane_index(shape):
    return lax.broadcasted_iota(jnp.int32, shape, len(shape) - 1)


def halves_of(per, planes):
    return 2 if per % planes == 0 and planes == 4 else 1


def pair_of_step(step, per, planes):
    if halves_of(per, planes) == 2:
        fields = per // planes
        return (step % fields) * planes + (3 * (step // fields)) % planes
    return step


def place_of_pair(pair, per, planes):
    held = per // halves_of(per, planes)
    steps = {pair_of_step(step, per, planes): step for step in range(per)}
    return divmod(steps[pair], held)


def move_kernel(
    count,
    rads,
    stages,
    orbit,
    state,
    main,
    ghost_cols,
    ghost_rows,
    side_cols,
    z_main,
    z_cols,
    z_rows,
    z_side,
    rows,
    turned,
    shift,
    out_cols,
    out_rows,
    send1,
    recv1,
    send2,
    recv2,
    send3,
    recv3,
    send4,
    recv4,
    own_sem,
):
    fields, planes, height, _ = main.shape
    per = fields * planes // count
    halves = halves_of(per, planes)
    held = per // halves
    sides = side_cols.shape[0]
    total = count * LANES
    tiles = height // 8
    group = lax.axis_index("groups")
    me = lax.axis_index("az")
    rad = lax.axis_index("rad")
    core = lax.axis_index("vert")
    up = (rad + 1) % rads
    down = (rad + rads - 1) % rads

    def device(az, r, v):
        return (group, az, r, v)

    barrier = pltpu.get_barrier_semaphore()
    targets = [device((me + d) % count, rad, core) for d in range(1, count)]
    for d in range(count):
        targets.append(device((me + d) % count, up, core))
        if sides > 1:
            targets.append(device((me + d) % count, down, core))
    targets.append(device(me, rad, 1 - core))
    for target in targets:
        pl.semaphore_signal(barrier, inc=1, device_id=target, device_id_type=MESH)

    own = pltpu.make_async_copy(state.at[pl.ds(me * per, per)], rows.at[me], own_sem.at[0])
    own.start()
    lane8 = lane_index((8, LANES))
    sub8 = lax.broadcasted_iota(jnp.int32, (8, LANES), 0)
    for t in range(tiles):
        amount = jnp.full((8, LANES), orbit[8 * t], jnp.int32)
        for i in range(1, 8):
            amount = jnp.where(sub8 == i, orbit[8 * t + i], amount)
        shift[pl.ds(8 * t, 8), :] = amount
    top = orbit[height - 1] + jnp.where(rad == rads - 1, orbit[height], 0)
    bottom = orbit[0] + jnp.where(rad == 0, total - orbit[height], 0)
    amount = jnp.where(sub8 == 7, top, bottom)
    shift[pl.ds(height, 8), :] = jnp.where(amount >= total, amount - total, amount)
    out_cols[...] = jnp.zeros_like(out_cols)
    pl.semaphore_wait(barrier, len(targets))

    def first(step, d):
        pair = pair_of_step(step, per, planes)
        peer = (me + d) % count
        return pltpu.make_async_remote_copy(
            src_ref=state.at[peer * per + pair],
            dst_ref=rows.at[me, pair],
            send_sem=send1.at[step, d],
            recv_sem=recv1.at[step, d],
            device_id=device(peer, rad, core),
            device_id_type=MESH,
        )

    def second(step, d):
        pair = pair_of_step(step, per, planes)
        peer = (me + d) % count
        whole = me * per + pair
        return pltpu.make_async_remote_copy(
            src_ref=turned.at[peer, pair],
            dst_ref=main.at[whole // planes, whole % planes],
            send_sem=send2.at[step, d],
            recv_sem=recv2.at[step, d],
            device_id=device(peer, rad, core),
            device_id_type=MESH,
        )

    def ghosts(half):
        copies = []
        base = half * 5 * count

        def add(source, target, slot, d, r):
            copies.append(
                pltpu.make_async_remote_copy(
                    src_ref=source,
                    dst_ref=target,
                    send_sem=send3.at[base + slot],
                    recv_sem=recv3.at[base + slot],
                    device_id=device((me + d) % count, r, core),
                    device_id_type=MESH,
                )
            )

        for d in range(count):
            peer = (me + d) % count
            if d > 0:
                add(out_cols.at[half, peer], ghost_cols.at[half, me], d, d, rad)
            for side in range(sides):
                r = up if side == sides - 1 else down
                slot = count + d * 4 + side * 2
                add(out_rows.at[half, peer], ghost_rows.at[side, half, me], slot, d, r)
                add(out_cols.at[half, peer], side_cols.at[side, half, me], slot + 1, d, r)
        return copies

    def start_first(step, carry):
        for d in range(1, count):
            first(step, d).start()
        return carry

    lax.fori_loop(0, per, start_first, 0)
    own.wait()
    bits = [bit for bit in range(31) if (1 << bit) < total]

    def turn(step, half):
        pair = pair_of_step(step, per, planes)
        slot = step - half * held
        for d in range(1, count):
            first(step, d).wait_recv()
        for t in range(tiles + 1):
            amount = shift[pl.ds(8 * t, 8), :]
            if t < tiles:
                blocks = [rows[b, pair, pl.ds(8 * t, 8), :] for b in range(count)]
            else:
                blocks = [
                    jnp.where(
                        sub8 == 7,
                        rows[b, pair, pl.ds(height - 1, 1), :],
                        rows[b, pair, pl.ds(0, 1), :],
                    )
                    for b in range(count)
                ]
            for bit in bits:
                if (1 << bit) < LANES:
                    continue
                q = (1 << bit) // LANES
                flag = ((amount >> bit) & 1) == 1
                blocks = [
                    jnp.where(flag, blocks[(b - q) % count], blocks[b]) for b in range(count)
                ]
            for bit in bits:
                if (1 << bit) >= LANES:
                    continue
                flag = ((amount >> bit) & 1) == 1
                blocks = [
                    jnp.where(flag, pltpu.roll(block, 1 << bit, 1), block) for block in blocks
                ]
            inside = lane8 >= (amount & (LANES - 1))
            out = [
                jnp.where(inside, blocks[b], blocks[(b - 1) % count]) for b in range(count)
            ]
            place = 2 * held * t + 2 * slot
            for b in range(count):
                low = jnp.broadcast_to(out[(b - 1) % count][:, LANES - 1 :], (8, LANES))
                high = jnp.broadcast_to(out[(b + 1) % count][:, :1], (8, LANES))
                out_cols[half, b] = jnp.where(
                    lane8 == place, low, jnp.where(lane8 == place + 1, high, out_cols[half, b])
                )
                if t < tiles:
                    turned[b, pair, pl.ds(8 * t, 8), :] = out[b]
                else:
                    out_rows[half, b, pl.ds(slot, 1), :] = out[b][0:1]
                    out_rows[half, b, pl.ds(held + slot, 1), :] = out[b][7:8]
        for d in range(1, count):
            second(step, d).start()
        whole = me * per + pair
        main[whole // planes, whole % planes] = turned[me, pair]

    small = []
    for half in range(halves):

        def body(step, carry, half=half):
            turn(step, half)
            return carry

        lax.fori_loop(half * held, (half + 1) * held, body, 0)
        small.append(ghosts(half))
        for copy in small[half]:
            copy.start()
        ghost_cols[half, me] = out_cols[half, me]

    def wait_second(step, carry):
        for d in range(1, count):
            second(step, d).wait_recv()
        return carry

    def across(index, source, target):
        return pltpu.make_async_remote_copy(
            src_ref=source,
            dst_ref=target,
            send_sem=send4.at[index],
            recv_sem=recv4.at[index],
            device_id=device(me, rad, 1 - core),
            device_id_type=MESH,
        )

    lax.fori_loop(0, held, wait_second, 0)
    for copy in small[0]:
        copy.wait_recv()
    last = [
        across(0, main.at[:, planes - 1], z_main.at[0]),
        across(1, main.at[:, 0], z_main.at[1]),
        across(2, ghost_cols.at[0], z_cols),
    ]
    for side in range(sides):
        last.append(across(3 + 2 * side, ghost_rows.at[side, 0], z_rows.at[side]))
        last.append(across(4 + 2 * side, side_cols.at[side, 0], z_side.at[side]))
    for copy in last:
        copy.start()
    stages[0]()
    for copy in last:
        copy.wait_recv()
    stages[1]()
    for half in range(1, halves):
        lax.fori_loop(half * held, (half + 1) * held, wait_second, 0)
        for copy in small[half]:
            copy.wait_recv()
    stages[2]()
    for copy in last:
        copy.wait_send()

    def finish(step, carry):
        for d in range(1, count):
            first(step, d).wait_send()
            second(step, d).wait_send()
        return carry

    lax.fori_loop(0, per, finish, 0)
    for half in range(halves):
        for copy in small[half]:
            copy.wait_send()


def primitives(cells):
    density, mx, my, mz, energy, bx, by, bz = cells
    inverse = 1.0 / density
    velocity = (mx * inverse, my * inverse, mz * inverse)
    magnet_sq = bx * bx + by * by + bz * bz
    kinetic = 0.5 * (mx * velocity[0] + my * velocity[1] + mz * velocity[2])
    pressure = (ADIABATIC - 1.0) * (energy - kinetic - 0.5 * magnet_sq)
    total_pressure = pressure + 0.5 * magnet_sq
    projection = velocity[0] * bx + velocity[1] * by + velocity[2] * bz
    fast_speed = jnp.sqrt((ADIABATIC * pressure + magnet_sq) * inverse)
    return velocity, total_pressure, projection, fast_speed


def one_flux(cells, prims, normal, piece):
    velocity, total_pressure, projection, _ = prims
    speed = velocity[normal]
    field = cells[5 + normal]
    if piece == 0:
        return cells[1 + normal]
    if piece < 4:
        value = cells[piece] * speed - cells[piece + 4] * field
        return value + total_pressure if piece == normal + 1 else value
    if piece == 4:
        return (cells[4] + total_pressure) * speed - field * projection
    return cells[piece] * speed - velocity[piece - 5] * field


def face_flux(left, left_prims, right, right_prims, normal, pieces):
    ls, lc = left_prims[0][normal], left_prims[3]
    rs, rc = right_prims[0][normal], right_prims[3]
    low = jnp.minimum(jnp.minimum(ls - lc, rs - rc), 0.0)
    high = jnp.maximum(jnp.maximum(ls + lc, rs + rc), 0.0)
    inverse = 1.0 / (high - low)
    wl = high * inverse
    wr = low * inverse
    wd = low * wl
    out = []
    for piece in pieces:
        if piece == 5 + normal:
            out.append(wd * (right[piece] - left[piece]))
            continue
        out.append(
            wl * one_flux(left, left_prims, normal, piece)
            - wr * one_flux(right, right_prims, normal, piece)
            + wd * (right[piece] - left[piece])
        )
    return out


def step_stages(
    count,
    main,
    ghost_cols,
    ghost_rows,
    side_cols,
    z_main,
    z_cols,
    z_rows,
    z_side,
    new,
    pad,
    cols,
    edge,
    fx7,
    fy7,
    fyr7,
    change,
    curl,
    zface,
    gy,
    gx6,
    gz6,
):
    fields, planes, height, _ = main.shape
    per = fields * planes // count
    tiles = height // 8
    tall = height + 8
    lane8 = lane_index((8, LANES))
    sub8 = lax.broadcasted_iota(jnp.int32, (8, LANES), 0)
    lane = lane_index((tall, LANES))
    padded = planes + 2

    sides = side_cols.shape[0]
    held = per // halves_of(per, planes)

    def source_of(f, p):
        k = (p - 1) % planes
        owner, pair = divmod(f * planes + k, per)
        half, slot = place_of_pair(pair, per, planes)
        return k, owner, half, slot

    def below(x):
        return pltpu.roll(x, 1, 0)

    def above(x):
        return pltpu.roll(x, tall - 1, 0)

    def assemble(chosen, fresh):
        for f in range(fields):
            for p in chosen:
                k, owner, half, slot = source_of(f, p)
                low, high = pl.ds(slot, 1), pl.ds(held + slot, 1)
                if 1 <= p <= planes:
                    pad[p, f, pl.ds(0, height)] = main[f, k]
                    before = ghost_rows[sides - 1, half, owner, high, :]
                    after = ghost_rows[0, half, owner, low, :]
                else:
                    pad[p, f, pl.ds(0, height)] = z_main[0 if p == 0 else 1, f]
                    before = z_rows[sides - 1, owner, high, :]
                    after = z_rows[0, owner, low, :]
                pad[p, f, pl.ds(height, 8)] = jnp.where(sub8 == 7, before, after)
            for t in range(tiles + 1):
                tile = jnp.zeros((8, LANES), jnp.float32) if fresh else cols[f, pl.ds(8 * t, 8)]
                for p in chosen:
                    k, owner, half, slot = source_of(f, p)
                    inner = 1 <= p <= planes
                    if t < tiles:
                        source = ghost_cols[half, owner] if inner else z_cols[owner]
                    elif inner:
                        source = jnp.where(
                            sub8 == 7, side_cols[sides - 1, half, owner], side_cols[0, half, owner]
                        )
                    else:
                        source = jnp.where(sub8 == 7, z_side[sides - 1, owner], z_side[0, owner])
                    moved = pltpu.roll(source, (2 * p - 2 * held * t - 2 * slot) % LANES, 1)
                    tile = jnp.where(lane8 // 2 == p, moved, tile)
                cols[f, pl.ds(8 * t, 8)] = tile
            tile = jnp.zeros((tall, LANES), jnp.float32) if fresh else edge[f]
            for p in chosen:
                tile = jnp.where(lane // 2 == p, pltpu.roll(pad[p, f], 2 * p + 2, 1), tile)
            edge[f] = tile

        ghost = [cols[f] for f in range(fields)]
        ghost_prims = primitives(ghost)
        last = [edge[f] for f in range(fields)]
        for piece, value in enumerate(
            face_flux(last, primitives(last), ghost, ghost_prims, 1, range(8))
        ):
            gy[piece] = value
        lower = [below(x) for x in ghost]
        gx6[...] = face_flux(lower, primitives(lower), ghost, ghost_prims, 0, (6,))[0]
        higher = [pltpu.roll(x, LANES - 2, 1) for x in ghost]
        gz6[...] = face_flux(ghost, ghost_prims, higher, primitives(higher), 2, (6,))[0]

    def left_of(x, ghosts, p):
        return jnp.where(lane == 0, pltpu.roll(ghosts, LANES - 2 * p, 1), pltpu.roll(x, 1, 1))

    def right_of(x, ghosts, p):
        return jnp.where(
            lane == LANES - 1,
            pltpu.roll(ghosts, LANES - 2 - 2 * p, 1),
            pltpu.roll(x, LANES - 1, 1),
        )

    def in_plane(p, carry):
        cells = [pad[p, f] for f in range(fields)]
        prims = primitives(cells)
        lower = [below(x) for x in cells]
        flux = face_flux(lower, primitives(lower), cells, prims, 0, range(8))
        fx7[p] = flux[7]
        for f in range(5):
            change[p, f] = (above(flux[f]) - flux[f])[:height]
        x6 = flux[6]
        side = [left_of(cells[f], cols[f], p) for f in range(fields)]
        flux = face_flux(side, primitives(side), cells, prims, 1, range(8))
        fy7[p] = flux[7]
        fyr7[p] = right_of(flux[7], gy[7], p)
        for f in range(5):
            change[p, f] += (right_of(flux[f], gy[f], p) - flux[f])[:height]
        y5 = flux[5]
        y5r = right_of(y5, gy[5], p)
        x6l = left_of(x6, gx6[...], p)
        x6r = right_of(x6, gx6[...], p)
        ez = 0.25 * (y5 + below(y5) - (x6 + x6l))
        ezr = 0.25 * (y5r + below(y5r) - (x6r + x6))
        ez_up = above(ez)
        ezr_up = above(ezr)
        curl[p, 0] = (0.5 * ((ezr_up + ezr) - (ez_up + ez)))[:height]
        curl[p, 1] = (0.5 * ((ezr_up + ez_up) - (ezr + ez)))[:height]
        return carry

    def between(q, carry):
        low = [pad[q, f] for f in range(fields)]
        high = [pad[q + 1, f] for f in range(fields)]
        flux = face_flux(low, primitives(low), high, primitives(high), 2, range(8))
        for f in range(5):
            zface[q, f] = flux[f][:height]
        z5, z6 = flux[5], flux[6]
        ey = 0.25 * (fx7[q + 1] + fx7[q] - (z5 + below(z5)))
        ex = 0.25 * (z6 + left_of(z6, gz6[...], q) - (fy7[q + 1] + fy7[q]))
        exr = 0.25 * (right_of(z6, gz6[...], q) + z6 - (fyr7[q + 1] + fyr7[q]))
        ey_up = above(ey)
        zface[q, 5] = (0.5 * (ey_up + ey))[:height]
        zface[q, 6] = (0.5 * (exr + ex))[:height]
        zface[q, 7] = (0.5 * ((ey_up - ey) - (exr - ex)))[:height]
        return carry

    def combine(k, carry):
        p = k + 1
        old = [pad[p, f, pl.ds(0, height)] for f in range(fields)]
        hydro = [
            old[f] - TIME_STEP * (change[p, f] + (zface[p, f] - zface[k, f])) for f in range(5)
        ]
        new[0, k] = hydro[0]
        new[1, k] = hydro[1] + TIME_STEP * 2.0 * ROTATION * old[2]
        new[2, k] = hydro[2] + TIME_STEP * (SHEAR_RATE - 2.0) * ROTATION * old[1]
        new[3, k] = hydro[3]
        new[4, k] = hydro[4]
        new[5, k] = old[5] - TIME_STEP * (curl[p, 0] - (zface[p, 5] - zface[k, 5]))
        new[6, k] = old[6] - TIME_STEP * ((zface[p, 6] - zface[k, 6]) - curl[p, 1])
        new[7, k] = old[7] - TIME_STEP * (zface[p, 7] + zface[k, 7])
        return carry

    def run(body, first, stride, times):
        lax.fori_loop(0, times, lambda i, carry: body(first + stride * i, carry), 0)

    early = halves_of(per, planes) == 2

    def outer():
        if early:
            assemble((1, planes), True)
            run(in_plane, 1, planes - 1, 2)

    def other_core():
        assemble((0, planes + 1), not early)
        run(in_plane, 0, planes + 1, 2)
        if early:
            run(between, 0, planes, 2)

    def inner():
        if early:
            assemble(tuple(range(2, planes)), False)
            run(in_plane, 2, 1, planes - 2)
            run(between, 1, 1, planes - 1)
        else:
            assemble(tuple(range(1, planes + 1)), False)
            run(in_plane, 1, 1, planes)
            run(between, 0, 1, planes + 1)
        run(combine, 0, 1, planes)

    return outer, other_core, inner


def whole_kernel(count, rads, orbit, state, new, *scratch):
    landed, rest, work = scratch[:8], scratch[8:22], scratch[22:]
    stages = step_stages(count, *landed, new, *work)
    move_kernel(count, rads, stages, orbit, state, *landed, *rest)


def per_device(state, orbit_shift, remap_shift):
    count = lax.axis_size("az")
    rads = lax.axis_size("rad")
    fields, planes, height, width = state.shape
    per = fields * planes // count
    halves = halves_of(per, planes)
    held = per // halves
    sides = 1 if rads == 2 else 2
    f32 = jnp.float32

    dma = pltpu.SemaphoreType.DMA
    tall = height + 8

    def held_in(*shape):
        return pltpu.VMEM(shape, f32)

    return pl.pallas_call(
        functools.partial(whole_kernel, count, rads),
        out_shape=jax.ShapeDtypeStruct(state.shape, f32),
        in_specs=[
            pl.BlockSpec(memory_space=pltpu.SMEM),
            pl.BlockSpec(memory_space=pl.ANY),
        ],
        out_specs=pl.BlockSpec(memory_space=pltpu.VMEM),
        scratch_shapes=[
            held_in(fields, planes, height, LANES),
            held_in(halves, count, 8, LANES),
            held_in(sides, halves, count, 2 * held, LANES),
            held_in(sides, halves, count, 8, LANES),
            held_in(2, fields, height, LANES),
            held_in(count, 8, LANES),
            held_in(sides, count, 2 * held, LANES),
            held_in(sides, count, 8, LANES),
            held_in(count, per, height, LANES),
            held_in(count, per, height, LANES),
            pltpu.VMEM((tall, LANES), jnp.int32),
            held_in(halves, count, 8, LANES),
            held_in(halves, count, 2 * held, LANES),
            dma((per, count)),
            dma((per, count)),
            dma((per, count)),
            dma((per, count)),
            dma((5 * count * halves,)),
            dma((5 * count * halves,)),
            dma((7,)),
            dma((7,)),
            dma((1,)),
            held_in(planes + 2, fields, tall, LANES),
            held_in(fields, tall, LANES),
            held_in(fields, tall, LANES),
            held_in(planes + 2, tall, LANES),
            held_in(planes + 2, tall, LANES),
            held_in(planes + 2, tall, LANES),
            held_in(planes + 2, 5, height, LANES),
            held_in(planes + 2, 2, height, LANES),
            held_in(planes + 1, 8, height, LANES),
            held_in(8, tall, LANES),
            held_in(tall, LANES),
            held_in(tall, LANES),
        ],
        compiler_params=pltpu.CompilerParams(
            collective_id=0, has_side_effects=True, vmem_limit_bytes=24 * 1024 * 1024
        ),
        name="whole",
    )(jnp.concatenate([orbit_shift, remap_shift]), state.reshape(fields * planes, height, width))


def solution(mesh):
    return jax.shard_map(
        per_device,
        mesh=mesh,
        in_specs=(P("groups", "vert", "rad", "az"), P(("groups", "rad")), P("groups")),
        out_specs=P("groups", "vert", "rad", "az"),
        check_vma=False,
    )
```
